128 devices in a mesh: outer: 16 (over z_hi, x, core), inner: 8 (over y, z_lo).
Axes of the slice: x: 4, y: 4, z: 4 (z_hi: 2, z_lo: 2; z = z_hi * 2 + z_lo), core: 2. Of those that a mesh axis runs over, the one named last changes fastest.
Arguments:
- queries: bfloat16 [32768, 1024], P(('outer', 'inner')), may hold values from -8 to 8
- keys: bfloat16 [32768, 1024], P(('outer', 'inner')), may hold values from -8 to 8
- values: bfloat16 [32768, 1024], P(('outer', 'inner')), may hold values from -6 to 6
- d_output: bfloat16 [32768, 1024], P(('outer', 'inner')), may hold values from -6 to 6
Outputs:
- grad_queries: bfloat16 [32768, 1024], P(('outer', 'inner'))
- grad_keys: bfloat16 [32768, 1024], P(('outer', 'inner'))
- grad_values: bfloat16 [32768, 1024], P(('outer', 'inner'))
The draws below stay inside these ranges and needn't reach their ends.
All inputs are finite; a program needn't handle non-finite values.
Results may differ from the reference program's by a relative error of at most 0.012.
The reference program's roundings to bfloat16 on the way (of `prob_low` and `dscore`) count: a program that leaves them out, or rounds other values in their place, can miss the bound.
Values may be sent and summed in bfloat16 or wider, within the bound.
A program may use at most 128 MiB of HBM per device.

```python
import jax
import jax.numpy as jnp
from jax import lax

D = 1024
HEADS = 16
HEAD_DIM = 64
TOK_DEV = 256
CYCLE_IN = 8
CYCLE_OUT = 16
TOKENS = 32768


def draw_queries(key, part):
    key = jax.random.fold_in(key, 11)
    base = jnp.clip(jax.random.normal(key, (TOKENS, D), jnp.float32), -6.0, 6.0)
    return base.astype(jnp.bfloat16)


def draw_keys(key, part):
    key = jax.random.fold_in(key, 23)
    base = jnp.clip(jax.random.normal(key, (TOKENS, D), jnp.float32), -6.0, 6.0)
    return base.astype(jnp.bfloat16)


def levels(rng, dims, split, smallest, largest):
    def one(dim, parts):
        heights = jax.random.uniform(jax.random.fold_in(jax.random.fold_in(rng, 6), dim), (parts,), jnp.float32, smallest / len(split), largest / len(split))
        return jnp.repeat(jnp.exp(heights), dims[dim] // parts).reshape((-1,) + (1,) * (len(dims) - dim - 1))

    factor_of = one(*split[0])
    for cut in split[1:]:
        factor_of = factor_of * one(*cut)
    return factor_of


def normal_values(rng, extent, scale, limit, cuts=(), held_as=jnp.bfloat16):
    drawn = scale * jax.random.normal(rng, extent, jnp.float32)
    if cuts:
        drawn = drawn * levels(rng, extent, cuts, -0.22, 0.18)
    return jnp.clip(drawn, -limit, limit).astype(held_as)


def setup_inputs(seed: int = 0) -> dict:
    splits = jax.random.split(jax.random.key(seed), 5)
    return {
        "queries": draw_queries(jax.random.fold_in(splits[4], 71), 0),
        "keys": draw_keys(jax.random.fold_in(splits[4], 71), 0),
        "values": normal_values(splits[2], (TOKENS, D), 1.0, 6.0, ((0, 128),)),
        "d_output": normal_values(splits[3], (TOKENS, D), 1.0, 6.0, ((0, 128),)),
    }


def window_grads(q_block, do_block, k_window, v_window):
    rows = q_block.shape[0]
    span = k_window.shape[0]
    scale = HEAD_DIM ** -0.5
    q_heads = q_block.reshape(rows, HEADS, HEAD_DIM).astype(jnp.float32)
    do_heads = do_block.reshape(rows, HEADS, HEAD_DIM).astype(jnp.float32)
    k_heads = k_window.reshape(span, HEADS, HEAD_DIM).astype(jnp.float32)
    v_heads = v_window.reshape(span, HEADS, HEAD_DIM).astype(jnp.float32)
    score = jnp.einsum("thd,shd->hts", q_heads, k_heads) * scale
    top = jnp.max(score, axis=-1, keepdims=True)
    lse = top + jnp.log(jnp.sum(jnp.exp(score - top), axis=-1, keepdims=True))
    prob = jnp.exp(score - lse)
    prob_low = prob.astype(jnp.bfloat16).astype(jnp.float32)
    output = jnp.einsum("hts,shd->thd", prob_low, v_heads)
    delta = jnp.transpose(jnp.sum(do_heads * output, axis=-1))
    dprob = jnp.einsum("thd,shd->hts", do_heads, v_heads)
    dscore = (prob * (dprob - delta[:, :, None])).astype(jnp.bfloat16).astype(jnp.float32)
    grad_q = jnp.einsum("hts,shd->thd", dscore, k_heads) * scale
    grad_k = jnp.einsum("hts,thd->shd", dscore, q_heads) * scale
    grad_v = jnp.einsum("hts,thd->shd", prob_low, do_heads)
    return grad_q.reshape(rows, D), grad_k.reshape(span, D), grad_v.reshape(span, D)


def reference(queries, keys, values, d_output):
    blocks = CYCLE_OUT * CYCLE_IN
    q_four = queries.reshape(CYCLE_OUT, CYCLE_IN, TOK_DEV, D)
    do_four = d_output.reshape(CYCLE_OUT, CYCLE_IN, TOK_DEV, D)
    k_four = keys.reshape(CYCLE_OUT, CYCLE_IN, TOK_DEV, D)
    v_four = values.reshape(CYCLE_OUT, CYCLE_IN, TOK_DEV, D)
    k_window = jnp.concatenate([k_four, jnp.roll(k_four, 1, axis=1), jnp.roll(k_four, 1, axis=0)], axis=2)
    v_window = jnp.concatenate([v_four, jnp.roll(v_four, 1, axis=1), jnp.roll(v_four, 1, axis=0)], axis=2)
    grad_q, grad_k, grad_v = lax.map(
        lambda item: window_grads(item[0], item[1], item[2], item[3]),
        (q_four.reshape(blocks, TOK_DEV, D), do_four.reshape(blocks, TOK_DEV, D),
         k_window.reshape(blocks, 3 * TOK_DEV, D), v_window.reshape(blocks, 3 * TOK_DEV, D)))
    grad_k = grad_k.reshape(CYCLE_OUT, CYCLE_IN, 3, TOK_DEV, D)
    grad_v = grad_v.reshape(CYCLE_OUT, CYCLE_IN, 3, TOK_DEV, D)
    total_k = grad_k[:, :, 0] + jnp.roll(grad_k[:, :, 1], -1, axis=1) + jnp.roll(grad_k[:, :, 2], -1, axis=0)
    total_v = grad_v[:, :, 0] + jnp.roll(grad_v[:, :, 1], -1, axis=1) + jnp.roll(grad_v[:, :, 2], -1, axis=0)
    return (grad_q.reshape(TOKENS, D).astype(jnp.bfloat16),
            total_k.reshape(TOKENS, D).astype(jnp.bfloat16),
            total_v.reshape(TOKENS, D).astype(jnp.bfloat16))
```

```python
import functools

import jax
import jax.numpy as jnp
from jax import lax
from jax.experimental import pallas as pl
from jax.experimental.pallas import tpu as pltpu
from jax.sharding import PartitionSpec as P

HEAD = 64
COLS = 128
MESH = pl.DeviceIdType.MESH
AHEAD = 2
LAG_C = 1
LAG_B = 2
LAG_E = 4
NT = (((1,), (1,)), ((), ()))


def kernel(
    outer_size, inner_size, groups, rows,
    q_hbm, k_hbm, v_hbm, do_hbm,
    dq_out, dk_out, dv_out,
    qd, kv, km, vm, kt, e_all, dp_all, p_low, ds_low,
    part, part_in, total, total_in, dq_own, dq_send, dq_in,
    load_sem, qd_send, qd_recv, part_send, part_recv,
    total_send, total_recv, dq_ssem, dq_rsem,
):
    o = lax.axis_index("outer")
    i = lax.axis_index("inner")
    before = [(o, lax.rem(i + inner_size - 1, inner_size)), (lax.rem(o + outer_size - 1, outer_size), i)]
    after = [(o, lax.rem(i + 1, inner_size)), (lax.rem(o + 1, outer_size), i)]

    def load_qd(g, which):
        src = (q_hbm, do_hbm)[which]
        return pltpu.make_async_copy(src.at[:, pl.ds(g * COLS, COLS)], qd.at[g, which, 0], load_sem.at[which, g])

    def load_kv(g, which):
        src = (k_hbm, v_hbm)[which]
        return pltpu.make_async_copy(src.at[:, pl.ds(g * COLS, COLS)], kv.at[g, which], load_sem.at[2 + which, g])

    def send_qd(g, r):
        return pltpu.make_async_remote_copy(
            qd.at[g, :, 0], qd.at[g, :, r + 1], qd_send.at[r, g], qd_recv.at[r, g],
            device_id=before[r], device_id_type=MESH)

    def send_part(g, r):
        return pltpu.make_async_remote_copy(
            part.at[g, r + 1], part_in.at[g, r], part_send.at[r, g], part_recv.at[r, g],
            device_id=after[r], device_id_type=MESH)

    def send_total(g, r):
        return pltpu.make_async_remote_copy(
            total.at[g], total_in.at[g, r], total_send.at[r, g], total_recv.at[r, g],
            device_id=before[r], device_id_type=MESH)

    def send_dq(g, r):
        return pltpu.make_async_remote_copy(
            dq_send.at[g, r], dq_in.at[g, r], dq_ssem.at[r, g], dq_rsem.at[r, g],
            device_id=after[r], device_id_type=MESH)

    for g in range(groups):
        for which in range(2):
            load_qd(g, which).start()
    for g in range(groups):
        for which in range(2):
            load_kv(g, which).start()

    barrier = pltpu.get_barrier_semaphore()
    for device in before + after:
        pl.semaphore_signal(barrier, inc=1, device_id=device, device_id_type=MESH)
    pl.semaphore_wait(barrier, 4)

    def start_group(g):
        for which in range(2):
            load_qd(g, which).wait()
        for r in range(2):
            send_qd(g, r).start()

    for g in range(AHEAD):
        start_group(g)

    lane = lax.broadcasted_iota(jnp.int32, (1, COLS), 1)
    first = lane < HEAD
    low = jnp.where(first, 1.0, 0.0)
    high = 1.0 - low
    scale = HEAD ** -0.5

    def prepare(g, carry):
        for which in range(2):
            load_kv(g, which).wait()
        k = kv[g, 0].astype(jnp.float32) * scale
        v = kv[g, 1].astype(jnp.float32)
        k_low, k_high = k * low, k * high
        km[g, 0] = k_low.astype(jnp.bfloat16)
        km[g, 1] = k_high.astype(jnp.bfloat16)
        vm[g, 0] = (v * low).astype(jnp.bfloat16)
        vm[g, 1] = (v * high).astype(jnp.bfloat16)
        kt[g, 0] = k_low.T.astype(jnp.bfloat16)
        kt[g, 1] = k_high.T.astype(jnp.bfloat16)
        return carry

    lax.fori_loop(0, groups, prepare, 0)

    def scores(g, r):
        q = qd[g, 0, r]
        do = qd[g, 1, r]
        for h in range(2):
            s = lax.dot_general(km[g, h], q, NT, preferred_element_type=jnp.float32)
            dp = lax.dot_general(vm[g, h], do, NT, preferred_element_type=jnp.float32)
            top = jnp.max(s, axis=0, keepdims=True)
            e = jnp.exp(s - top)
            e_all[g, r, h] = e
            dp_all[g, r, h] = dp
            part[g, r, pl.ds(h, 1)] = top
            part[g, r, pl.ds(2 + h, 1)] = jnp.sum(e, axis=0, keepdims=True)
            part[g, r, pl.ds(4 + h, 1)] = jnp.sum(e * dp, axis=0, keepdims=True)

    def combine(g):
        for r in range(2):
            send_part(g, r).wait_recv()
        parts = [part[g, 0], part_in[g, 0], part_in[g, 1]]
        tops = [x[0:2] for x in parts]
        top = jnp.maximum(jnp.maximum(tops[0], tops[1]), tops[2])
        weights = [jnp.exp(x - top) for x in tops]
        norm = sum(w * x[2:4] for w, x in zip(weights, parts))
        dots = sum(w * x[4:6] for w, x in zip(weights, parts))
        total[g, 0:2] = top + jnp.log(norm)
        total[g, 2:4] = dots / norm
        for r in range(2):
            send_total(g, r).start()

    def gradients(g):
        for r in range(2):
            send_total(g, r).wait_recv()
        for r in (1, 2, 0):
            sums = total[g] if r == 0 else total_in[g, r - 1]
            for h in range(2):
                factor = jnp.exp(part[g, r, pl.ds(h, 1)] - sums[h:h + 1])
                p = e_all[g, r, h] * factor
                p_low[h, :, r * rows:(r + 1) * rows] = p.astype(jnp.bfloat16)
                ds = p * (dp_all[g, r, h] - sums[2 + h:3 + h])
                ds_low[h, :, r * rows:(r + 1) * rows] = ds.astype(jnp.bfloat16)
            columns = slice(r * rows, (r + 1) * rows)
            dq = jnp.dot(kt[g, 0], ds_low[0, :, columns], preferred_element_type=jnp.float32)
            dq = dq + jnp.dot(kt[g, 1], ds_low[1, :, columns], preferred_element_type=jnp.float32)
            if r == 0:
                dq_own[g] = dq
            else:
                dq_send[g, r - 1] = dq.astype(jnp.bfloat16)
                send_dq(g, r - 1).start()
        columns = pl.ds(pl.multiple_of(g * COLS, COLS), COLS)
        q = qd[g, 0].reshape(3 * rows, COLS)
        do = qd[g, 1].reshape(3 * rows, COLS)
        dv = [jnp.dot(p_low[h], do, preferred_element_type=jnp.float32) for h in range(2)]
        dv_out[:, columns] = jnp.where(first, dv[0], dv[1]).astype(jnp.bfloat16)
        dk = [jnp.dot(ds_low[h], q, preferred_element_type=jnp.float32) for h in range(2)]
        dk_out[:, columns] = (jnp.where(first, dk[0], dk[1]) * scale).astype(jnp.bfloat16)

    def finish(g):
        for r in range(2):
            send_dq(g, r).wait_recv()
        dq = dq_own[g] + dq_in[g, 0].astype(jnp.float32) + dq_in[g, 1].astype(jnp.float32)
        columns = pl.ds(pl.multiple_of(g * COLS, COLS), COLS)
        dq_out[:, columns] = dq.T.astype(jnp.bfloat16)

    def step(t, carry):
        @pl.when(t < groups)
        def _():
            scores(t, 0)
            for r in (1, 0):
                send_qd(t, r).wait_recv()
                scores(t, r + 1)
                send_part(t, r).start()

        @pl.when(t < groups - AHEAD)
        def _():
            start_group(t + AHEAD)

        @pl.when((t >= LAG_C) & (t < groups + LAG_C))
        def _():
            combine(t - LAG_C)

        @pl.when((t >= LAG_B) & (t < groups + LAG_B))
        def _():
            gradients(t - LAG_B)

        @pl.when((t >= LAG_E) & (t < groups + LAG_E))
        def _():
            finish(t - LAG_E)

        return carry

    lax.fori_loop(0, groups + max(LAG_B, LAG_C, LAG_E), step, 0)

    def drain(g, carry):
        for r in range(2):
            send_qd(g, r).wait_send()
            send_part(g, r).wait_send()
            send_total(g, r).wait_send()
            send_dq(g, r).wait_send()
        return carry

    lax.fori_loop(0, groups, drain, 0)


def local(outer_size, inner_size, queries, keys, values, d_output):
    rows, width = queries.shape
    groups = width // COLS
    block = jax.ShapeDtypeStruct((rows, width), jnp.bfloat16)
    low, wide = jnp.bfloat16, jnp.float32
    dma = pltpu.SemaphoreType.DMA
    return pl.pallas_call(
        functools.partial(kernel, outer_size, inner_size, groups, rows),
        out_shape=(block, block, block),
        in_specs=[pl.BlockSpec(memory_space=pl.ANY)] * 4,
        out_specs=[pl.BlockSpec(memory_space=pltpu.VMEM)] * 3,
        scratch_shapes=[
            pltpu.VMEM((groups, 2, 3, rows, COLS), low),
            pltpu.VMEM((groups, 2, rows, COLS), low),
            pltpu.VMEM((groups, 2, rows, COLS), low),
            pltpu.VMEM((groups, 2, rows, COLS), low),
            pltpu.VMEM((groups, 2, COLS, rows), low),
            pltpu.VMEM((groups, 3, 2, rows, rows), wide),
            pltpu.VMEM((groups, 3, 2, rows, rows), wide),
            pltpu.VMEM((2, rows, 3 * rows), low),
            pltpu.VMEM((2, rows, 3 * rows), low),
            pltpu.VMEM((groups, 3, 8, rows), wide),
            pltpu.VMEM((groups, 2, 8, rows), wide),
            pltpu.VMEM((groups, 8, rows), wide),
            pltpu.VMEM((groups, 2, 8, rows), wide),
            pltpu.VMEM((groups, COLS, rows), wide),
            pltpu.VMEM((groups, 2, COLS, rows), low),
            pltpu.VMEM((groups, 2, COLS, rows), low),
            dma((4, groups)),
            dma((2, groups)), dma((2, groups)),
            dma((2, groups)), dma((2, groups)),
            dma((2, groups)), dma((2, groups)),
            dma((2, groups)), dma((2, groups)),
        ],
        compiler_params=pltpu.CompilerParams(
            collective_id=0, has_side_effects=True, vmem_limit_bytes=58 * 2**20),
    )(queries, keys, values, d_output)


def solution(mesh):
    spec = P(("outer", "inner"), None)
    return jax.shard_map(
        functools.partial(local, mesh.shape["outer"], mesh.shape["inner"]),
        mesh=mesh, in_specs=(spec,) * 4, out_specs=(spec,) * 3, check_vma=False)
```

```python
import functools

import jax
import jax.numpy as jnp
from jax import lax
from jax.experimental import pallas as pl
from jax.experimental.pallas import tpu as pltpu
from jax.sharding import PartitionSpec as P

HEAD = 64
COLS = 128
MESH = pl.DeviceIdType.MESH
AHEAD = 2
BATCHES = ((0, 4), (4, 4))
COMBINE = (5, 8)
LAG_B = 6
LAG_K = 10
LAG_E = 10
BACK_LAG = 2
HOP_LEAD = 1
NT = (((1,), (1,)), ((), ()))
RELAYS = {2: (1, 3, 6), 4: (2, 4, 7)}
RELAYED = sum(RELAYS.values(), ())
BACK = {}
BACKED = sum(BACK.values(), ())


def kernel(
    outer_size, inner_size, groups, rows,
    q_hbm, k_hbm, v_hbm, do_hbm,
    dq_out, dk_out, dv_out,
    qd, kv, km, vm, kt, e_all, dp_all, p_low, ds_low,
    part, part_in, total, total_in, dq_own, dq_send, dq_in, passing, passing_back,
    load_sem, qd_send, qd_recv, part_send, part_recv,
    total_send, total_recv, dq_ssem, dq_rsem, hop_send, hop_recv, pass_send,
    back_recv, back_send,
):
    o = lax.axis_index("outer")
    i = lax.axis_index("inner")
    before = [(o, lax.rem(i + inner_size - 1, inner_size)), (lax.rem(o + outer_size - 1, outer_size), i)]
    after = [(o, lax.rem(i + 1, inner_size)), (lax.rem(o + 1, outer_size), i)]

    def load_qd(g, which):
        src = (q_hbm, do_hbm)[which]
        return pltpu.make_async_copy(src.at[:, pl.ds(g * COLS, COLS)], qd.at[g, which, 0], load_sem.at[which, g])

    def load_kv(g, which):
        src = (k_hbm, v_hbm)[which]
        return pltpu.make_async_copy(src.at[:, pl.ds(g * COLS, COLS)], kv.at[g, which], load_sem.at[2 + which, g])

    def send_qd(g, r):
        return pltpu.make_async_remote_copy(
            qd.at[g, :, 0], qd.at[g, :, r + 1], qd_send.at[r, g], qd_recv.at[r, g],
            device_id=before[r], device_id_type=MESH)

    half = outer_size // 2
    place = lax.rem(o, half)
    base = o - place
    other = lax.rem(base + half, outer_size)
    wraps = place == 0

    def hop_in(g, slot, relay):
        return pltpu.make_async_remote_copy(
            qd.at[g, :, 0], passing.at[slot], hop_send.at[g], hop_recv.at[slot],
            device_id=(other + relay, i), device_id_type=MESH)

    def hop_out(g, slot):
        return pltpu.make_async_remote_copy(
            passing.at[slot], qd.at[g, :, 2], pass_send.at[slot], qd_recv.at[1, g],
            device_id=(base + half - 1, i), device_id_type=MESH)

    def back_in(g, slot, relay):
        return pltpu.make_async_remote_copy(
            dq_send.at[g, 1], passing_back.at[slot], dq_ssem.at[1, g], back_recv.at[slot],
            device_id=(other + relay, i), device_id_type=MESH)

    def back_out(g, slot):
        return pltpu.make_async_remote_copy(
            passing_back.at[slot], dq_in.at[g, 1], back_send.at[slot], dq_rsem.at[1, g],
            device_id=(base, i), device_id_type=MESH)

    def send_part(b, r):
        batch = pl.ds(*BATCHES[b])
        return pltpu.make_async_remote_copy(
            part.at[r + 1, batch], part_in.at[r, batch], part_send.at[r, b], part_recv.at[r, b],
            device_id=after[r], device_id_type=MESH)

    def send_total(b, r):
        batch = pl.ds(*BATCHES[b])
        return pltpu.make_async_remote_copy(
            total.at[batch], total_in.at[r, batch], total_send.at[r, b], total_recv.at[r, b],
            device_id=before[r], device_id_type=MESH)

    def send_dq(g, r):
        return pltpu.make_async_remote_copy(
            dq_send.at[g, r], dq_in.at[g, r], dq_ssem.at[r, g], dq_rsem.at[r, g],
            device_id=after[r], device_id_type=MESH)

    for g in range(groups):
        for which in range(2):
            load_qd(g, which).start()
    for g in range(groups):
        for which in range(2):
            load_kv(g, which).start()

    barrier = pltpu.get_barrier_semaphore()
    for device in before + after:
        pl.semaphore_signal(barrier, inc=1, device_id=device, device_id_type=MESH)
    peers = {n: 4 for n in range(half)}
    for relay in RELAYS:
        @pl.when(place == relay)
        def _():
            pl.semaphore_signal(barrier, inc=1, device_id=(other, i), device_id_type=MESH)

        @pl.when(place == half - 1)
        def _():
            pl.semaphore_signal(barrier, inc=1, device_id=(base + relay, i), device_id_type=MESH)

        peers[0] += 1
        peers[relay] += 1
    for relay in BACK:
        @pl.when(place == relay)
        def _():
            pl.semaphore_signal(barrier, inc=1, device_id=(other + half - 1, i), device_id_type=MESH)

        @pl.when(place == 0)
        def _():
            pl.semaphore_signal(barrier, inc=1, device_id=(base + relay, i), device_id_type=MESH)

        peers[half - 1] += 1
        peers[relay] += 1
    for count in sorted(set(peers.values())):
        @pl.when(functools.reduce(lambda a, b: a | b, [place == n for n in range(half) if peers[n] == count]))
        def _():
            pl.semaphore_wait(barrier, count)

    def among(g, listed):
        return functools.reduce(lambda a, b: a | b, [g == n for n in listed], g < 0)

    def start_group(g):
        send_qd(g, 0).start()

        @pl.when(jnp.logical_not(wraps & among(g, RELAYED)))
        def _():
            send_qd(g, 1).start()

    for g in range(groups):
        for which in range(2):
            load_qd(g, which).wait()
        if g < AHEAD:
            start_group(jnp.int32(g))

    @pl.when(wraps)
    def _():
        for g in sorted(RELAYED):
            for relay, listed in RELAYS.items():
                if g in listed:
                    hop_in(g, listed.index(g), relay).start()

    lane = lax.broadcasted_iota(jnp.int32, (1, COLS), 1)
    first = lane < HEAD
    low = jnp.where(first, 1.0, 0.0)
    high = 1.0 - low
    scale = HEAD ** -0.5

    def prepare(g, carry):
        for which in range(2):
            load_kv(g, which).wait()
        k = kv[g, 0].astype(jnp.float32) * scale
        v = kv[g, 1].astype(jnp.float32)
        k_low, k_high = k * low, k * high
        km[g, 0] = k_low.astype(jnp.bfloat16)
        km[g, 1] = k_high.astype(jnp.bfloat16)
        vm[g, 0] = (v * low).astype(jnp.bfloat16)
        vm[g, 1] = (v * high).astype(jnp.bfloat16)
        kt[g, 0] = k_low.T.astype(jnp.bfloat16)
        kt[g, 1] = k_high.T.astype(jnp.bfloat16)
        return carry

    lax.fori_loop(0, groups, prepare, 0)

    def scores(g, r):
        q = qd[g, 0, r]
        do = qd[g, 1, r]
        for h in range(2):
            s = lax.dot_general(km[g, h], q, NT, preferred_element_type=jnp.float32)
            dp = lax.dot_general(vm[g, h], do, NT, preferred_element_type=jnp.float32)
            top = jnp.max(s, axis=0, keepdims=True)
            e = jnp.exp(s - top)
            e_all[g, r, h] = e
            dp_all[g, r, h] = dp
            part[r, g, pl.ds(h, 1)] = top
            part[r, g, pl.ds(2 + h, 1)] = jnp.sum(e, axis=0, keepdims=True)
            part[r, g, pl.ds(4 + h, 1)] = jnp.sum(e * dp, axis=0, keepdims=True)

    def combine(b):
        for r in range(2):
            send_part(b, r).wait_recv()

        def one(g, carry):
            parts = [part[0, g], part_in[0, g], part_in[1, g]]
            tops = [x[0:2] for x in parts]
            top = jnp.maximum(jnp.maximum(tops[0], tops[1]), tops[2])
            weights = [jnp.exp(x - top) for x in tops]
            norm = sum(w * x[2:4] for w, x in zip(weights, parts))
            dots = sum(w * x[4:6] for w, x in zip(weights, parts))
            total[g, 0:2] = top + jnp.log(norm)
            total[g, 2:4] = dots / norm
            return carry

        first, count = BATCHES[b]
        lax.fori_loop(first, first + count, one, 0)
        for r in range(2):
            send_total(b, r).start()

    def gradients(g):
        for b in range(len(BATCHES)):
            @pl.when(g == BATCHES[b][0])
            def _():
                for r in range(2):
                    send_total(b, r).wait_recv()
        for r in (1, 2, 0):
            sums = total[g] if r == 0 else total_in[r - 1, g]
            for h in range(2):
                factor = jnp.exp(part[r, g, pl.ds(h, 1)] - sums[h:h + 1])
                p = e_all[g, r, h] * factor
                p_low[g, h, :, r * rows:(r + 1) * rows] = p.astype(jnp.bfloat16)
                ds = p * (dp_all[g, r, h] - sums[2 + h:3 + h])
                ds_low[g, h, :, r * rows:(r + 1) * rows] = ds.astype(jnp.bfloat16)
            columns = slice(r * rows, (r + 1) * rows)
            dq = jnp.dot(kt[g, 0], ds_low[g, 0, :, columns], preferred_element_type=jnp.float32)
            dq = dq + jnp.dot(kt[g, 1], ds_low[g, 1, :, columns], preferred_element_type=jnp.float32)
            if r == 0:
                dq_own[g] = dq
            else:
                dq_send[g, r - 1] = dq.astype(jnp.bfloat16)
                if r == 1:
                    send_dq(g, 0).start()
                else:
                    @pl.when(jnp.logical_not((place == half - 1) & among(g, BACKED)))
                    def _():
                        send_dq(g, 1).start()

                    for relay, listed in BACK.items():
                        for slot, n in enumerate(listed):
                            @pl.when((place == half - 1) & (g == n))
                            def _():
                                back_in(n, slot, relay).start()
    def key_gradients(g):
        columns = pl.ds(pl.multiple_of(g * COLS, COLS), COLS)
        q = qd[g, 0].reshape(3 * rows, COLS)
        do = qd[g, 1].reshape(3 * rows, COLS)
        dv = [jnp.dot(p_low[g, h], do, preferred_element_type=jnp.float32) for h in range(2)]
        dv_out[:, columns] = jnp.where(first, dv[0], dv[1]).astype(jnp.bfloat16)
        dk = [jnp.dot(ds_low[g, h], q, preferred_element_type=jnp.float32) for h in range(2)]
        dk_out[:, columns] = (jnp.where(first, dk[0], dk[1]) * scale).astype(jnp.bfloat16)

    def finish(g):
        for r in range(2):
            send_dq(g, r).wait_recv()
        dq = dq_own[g] + dq_in[g, 0].astype(jnp.float32) + dq_in[g, 1].astype(jnp.float32)
        columns = pl.ds(pl.multiple_of(g * COLS, COLS), COLS)
        dq_out[:, columns] = dq.T.astype(jnp.bfloat16)

    def step(t, carry):
        @pl.when(t < groups)
        def _():
            scores(t, 0)
            send_qd(t, 1).wait_recv()
            scores(t, 2)

        for relay, listed in RELAYS.items():
            for slot, g in enumerate(listed):
                @pl.when((place == relay) & (t == g - HOP_LEAD))
                def _():
                    hop_in(g, slot, relay).wait_recv()
                    hop_out(g, slot).start()

        @pl.when(t < groups)
        def _():
            send_qd(t, 0).wait_recv()
            scores(t, 1)

        for b in range(len(BATCHES)):
            @pl.when(t == sum(BATCHES[b]) - 1)
            def _():
                for r in range(2):
                    send_part(b, r).start()

        @pl.when(t < groups - AHEAD)
        def _():
            start_group(t + AHEAD)

        for b in range(len(BATCHES)):
            @pl.when(t == COMBINE[b])
            def _():
                combine(b)

        @pl.when((t >= LAG_B) & (t < groups + LAG_B))
        def _():
            gradients(t - LAG_B)

        for relay, listed in BACK.items():
            for slot, n in enumerate(listed):
                @pl.when((place == relay) & (t == n + LAG_B + BACK_LAG))
                def _():
                    back_in(n, slot, relay).wait_recv()
                    back_out(n, slot).start()

        @pl.when((t >= LAG_K) & (t < groups + LAG_K))
        def _():
            key_gradients(t - LAG_K)

        @pl.when((t >= LAG_E) & (t < groups + LAG_E))
        def _():
            finish(t - LAG_E)

        return carry

    lax.fori_loop(0, groups + max(LAG_K, LAG_E), step, 0)

    def drain(g, carry):
        for r in range(2):
            send_dq(g, r).wait_send()
        send_qd(g, 0).wait_send()

        @pl.when(jnp.logical_not(wraps & among(g, RELAYED)))
        def _():
            send_qd(g, 1).wait_send()

        return carry

    lax.fori_loop(0, groups, drain, 0)
    for relay, listed in BACK.items():
        for slot, g in enumerate(listed):
            @pl.when(place == relay)
            def _():
                back_out(g, slot).wait_send()

    for relay, listed in RELAYS.items():
        for slot, g in enumerate(listed):
            @pl.when(wraps)
            def _():
                hop_in(g, slot, relay).wait_send()

            @pl.when(place == relay)
            def _():
                hop_out(g, slot).wait_send()

    for b in range(len(BATCHES)):
        for r in range(2):
            send_part(b, r).wait_send()
            send_total(b, r).wait_send()


def copy_kernel(*refs):
    count = len(refs) // 3
    sems = refs[-1]
    ins, outs, held = refs[:count], refs[count:2 * count], refs[2 * count:3 * count]
    loads = [pltpu.make_async_copy(ins[n], held[n], sems.at[0, n]) for n in range(count)]
    stores = [pltpu.make_async_copy(held[n], outs[n], sems.at[1, n]) for n in range(count)]
    for load in loads:
        load.start()
    for load, store in zip(loads, stores):
        load.wait()
        store.start()
    for store in stores:
        store.wait()


def local(outer_size, inner_size, queries, keys, values, d_output):
    rows, width = queries.shape
    groups = width // COLS
    block = jax.ShapeDtypeStruct((rows, width), jnp.bfloat16)
    low, wide = jnp.bfloat16, jnp.float32
    dma = pltpu.SemaphoreType.DMA
    grads = pl.pallas_call(
        functools.partial(kernel, outer_size, inner_size, groups, rows),
        out_shape=(block, block, block),
        in_specs=[pl.BlockSpec(memory_space=pl.ANY)] * 4,
        out_specs=[pl.BlockSpec(memory_space=pltpu.VMEM)] * 3,
        scratch_shapes=[
            pltpu.VMEM((groups, 2, 3, rows, COLS), low),
            pltpu.VMEM((groups, 2, rows, COLS), low),
            pltpu.VMEM((groups, 2, rows, COLS), low),
            pltpu.VMEM((groups, 2, rows, COLS), low),
            pltpu.VMEM((groups, 2, COLS, rows), low),
            pltpu.VMEM((groups, 3, 2, rows, rows), wide),
            pltpu.VMEM((groups, 3, 2, rows, rows), wide),
            pltpu.VMEM((groups, 2, rows, 3 * rows), low),
            pltpu.VMEM((groups, 2, rows, 3 * rows), low),
            pltpu.VMEM((3, groups, 8, rows), wide),
            pltpu.VMEM((2, groups, 8, rows), wide),
            pltpu.VMEM((groups, 8, rows), wide),
            pltpu.VMEM((2, groups, 8, rows), wide),
            pltpu.VMEM((groups, COLS, rows), wide),
            pltpu.VMEM((groups, 2, COLS, rows), low),
            pltpu.VMEM((groups, 2, COLS, rows), low),
            pltpu.VMEM((3, 2, rows, COLS), low),
            pltpu.VMEM((2, COLS, rows), low),
            dma((4, groups)),
            dma((2, groups)), dma((2, groups)),
            dma((2, groups)), dma((2, groups)),
            dma((2, groups)), dma((2, groups)),
            dma((2, groups)), dma((2, groups)),
            dma((groups,)), dma((3,)), dma((3,)),
            dma((2,)), dma((2,)),
        ],
        compiler_params=pltpu.CompilerParams(
            collective_id=0, has_side_effects=True, vmem_limit_bytes=58 * 2**20),
    )(queries, keys, values, d_output)
    return pl.pallas_call(
        copy_kernel,
        out_shape=(block, block, block),
        in_specs=[pl.BlockSpec(memory_space=pl.ANY)] * 3,
        out_specs=[pl.BlockSpec(memory_space=pl.ANY)] * 3,
        scratch_shapes=[pltpu.VMEM((rows, width), low)] * 3 + [dma((2, 3))],
    )(*grads)


def solution(mesh):
    spec = P(("outer", "inner"), None)
    return jax.shard_map(
        functools.partial(local, mesh.shape["outer"], mesh.shape["inner"]),
        mesh=mesh, in_specs=(spec,) * 4, out_specs=(spec,) * 3, check_vma=False)
```

```python
import functools

import jax
import jax.numpy as jnp
from jax import lax
from jax.experimental import pallas as pl
from jax.experimental.pallas import tpu as pltpu
from jax.sharding import PartitionSpec as P

HEAD = 64
COLS = 128
MESH = pl.DeviceIdType.MESH
AHEAD = 2
BATCHES = ((0,4),(4,2),(6,2))
LAG_B = 6
LAG_K = 7
LAG_E = 8
HOP_LEAD = 1
NT = (((1,), (1,)), ((), ()))
RELAYS = {2: (1, 3, 6), 4: (2, 4, 7)}
RELAYED = sum(RELAYS.values(), ())


def kernel(
    outer_size, inner_size, groups, rows,
    q_hbm, k_hbm, v_hbm, do_hbm,
    dq_out, dk_out, dv_out,
    qd, kv, km, vm, kt, e_all, dp_all, p_low, ds_low,
    part, stats, stats_in, dq_own, dq_send, dq_in, passing,
    load_sem, qd_send, qd_recv, stats_send, stats_recv,
    dq_ssem, dq_rsem, hop_send, hop_recv, pass_send,
):
    o = lax.axis_index("outer")
    i = lax.axis_index("inner")
    before = [(o, lax.rem(i + inner_size - 1, inner_size)), (lax.rem(o + outer_size - 1, outer_size), i)]
    after = [(o, lax.rem(i + 1, inner_size)), (lax.rem(o + 1, outer_size), i)]
    across = [(before[1][0], after[0][1]), (after[1][0], before[0][1])]

    def load_qd(g, which):
        src = (q_hbm, do_hbm)[which]
        return pltpu.make_async_copy(src.at[:, pl.ds(g * COLS, COLS)], qd.at[g, which, 0], load_sem.at[which, g])

    def load_kv(g, which):
        src = (k_hbm, v_hbm)[which]
        return pltpu.make_async_copy(src.at[:, pl.ds(g * COLS, COLS)], kv.at[g, which], load_sem.at[2 + which, g])

    def send_qd(g, r):
        return pltpu.make_async_remote_copy(
            qd.at[g, :, 0], qd.at[g, :, r + 1], qd_send.at[r, g], qd_recv.at[r, g],
            device_id=before[r], device_id_type=MESH)

    half = outer_size // 2
    place = lax.rem(o, half)
    base = o - place
    other = lax.rem(base + half, outer_size)
    wraps = place == 0

    def hop_in(g, slot, relay):
        return pltpu.make_async_remote_copy(
            qd.at[g, :, 0], passing.at[slot], hop_send.at[g], hop_recv.at[slot],
            device_id=(other + relay, i), device_id_type=MESH)

    def hop_out(g, slot):
        return pltpu.make_async_remote_copy(
            passing.at[slot], qd.at[g, :, 2], pass_send.at[slot], qd_recv.at[1, g],
            device_id=(base + half - 1, i), device_id_type=MESH)

    routes = (
        (0, before[0], 1, 0),
        (1, after[0], 0, 0),
        (1, across[0], 2, 1),
        (2, across[1], 1, 1),
        (0, before[1], 2, 0),
        (2, after[1], 0, 1),
    )

    def send_stats(b, n):
        r, device, there, place_there = routes[n]
        start, count = BATCHES[b]
        pairs = pl.ds(start // 2, count // 2)
        return pltpu.make_async_remote_copy(
            stats.at[r, pairs], stats_in.at[there, place_there, pairs], stats_send.at[n, b], stats_recv.at[n, b],
            device_id=device, device_id_type=MESH)

    def send_dq(g, r):
        return pltpu.make_async_remote_copy(
            dq_send.at[g, r], dq_in.at[g, r], dq_ssem.at[r, g], dq_rsem.at[r, g],
            device_id=after[r], device_id_type=MESH)

    for g in range(groups):
        for which in range(2):
            load_qd(g, which).start()
    for g in range(groups):
        for which in range(2):
            load_kv(g, which).start()

    barrier = pltpu.get_barrier_semaphore()
    for device in before + after + across:
        pl.semaphore_signal(barrier, inc=1, device_id=device, device_id_type=MESH)
    peers = {n: 6 for n in range(half)}
    for relay in RELAYS:
        @pl.when(place == relay)
        def _():
            pl.semaphore_signal(barrier, inc=1, device_id=(other, i), device_id_type=MESH)

        @pl.when(place == half - 1)
        def _():
            pl.semaphore_signal(barrier, inc=1, device_id=(base + relay, i), device_id_type=MESH)

        peers[0] += 1
        peers[relay] += 1
    for count in sorted(set(peers.values())):
        @pl.when(functools.reduce(lambda a, b: a | b, [place == n for n in range(half) if peers[n] == count]))
        def _():
            pl.semaphore_wait(barrier, count)

    def among(g, listed):
        return functools.reduce(lambda a, b: a | b, [g == n for n in listed], g < 0)

    def start_group(g):
        send_qd(g, 0).start()

        @pl.when(jnp.logical_not(wraps & among(g, RELAYED)))
        def _():
            send_qd(g, 1).start()

    for g in range(groups):
        for which in range(2):
            load_qd(g, which).wait()
        if g < AHEAD:
            start_group(jnp.int32(g))

    @pl.when(wraps)
    def _():
        for g in sorted(RELAYED):
            for relay, listed in RELAYS.items():
                if g in listed:
                    hop_in(g, listed.index(g), relay).start()

    lane = lax.broadcasted_iota(jnp.int32, (1, COLS), 1)
    first = lane < HEAD
    low = jnp.where(first, 1.0, 0.0)
    high = 1.0 - low
    scale = HEAD ** -0.5

    def prepare(g, carry):
        for which in range(2):
            load_kv(g, which).wait()
        k = kv[g, 0].astype(jnp.float32) * scale
        v = kv[g, 1].astype(jnp.float32)
        k_low, k_high = k * low, k * high
        km[g, 0] = k_low.astype(jnp.bfloat16)
        km[g, 1] = k_high.astype(jnp.bfloat16)
        vm[g, 0] = (v * low).astype(jnp.bfloat16)
        vm[g, 1] = (v * high).astype(jnp.bfloat16)
        kt[g, 0] = k_low.T.astype(jnp.bfloat16)
        kt[g, 1] = k_high.T.astype(jnp.bfloat16)
        return carry

    lax.fori_loop(0, groups, prepare, 0)

    def scores(g, r):
        q = qd[g, 0, r]
        do = qd[g, 1, r]
        for h in range(2):
            s = lax.dot_general(km[g, h], q, NT, preferred_element_type=jnp.float32)
            dp = lax.dot_general(vm[g, h], do, NT, preferred_element_type=jnp.float32)
            top = jnp.max(s, axis=0, keepdims=True)
            e = jnp.exp(s - top)
            e_all[g, r, h] = e
            dp_all[g, r, h] = dp
            norm = jnp.sum(e, axis=0, keepdims=True)
            part[r, g, pl.ds(h, 1)] = top + jnp.log(norm)
            part[r, g, pl.ds(2 + h, 1)] = jnp.sum(e * dp, axis=0, keepdims=True) / norm
            part[r, g, pl.ds(4 + h, 1)] = top

    def share(b):
        start, count = BATCHES[b]
        for r in range(3):
            for g in range(start, start + count, 2):
                stats[r, g // 2, 0:4] = part[r, g, 0:4]
                stats[r, g // 2, 4:8] = part[r, g + 1, 0:4]
        for n in range(len(routes)):
            send_stats(b, n).start()

    def gradients(g):
        for b in range(len(BATCHES)):
            @pl.when(g == BATCHES[b][0])
            def _():
                for n in range(len(routes)):
                    send_stats(b, n).wait_recv()

        odd = lax.rem(g, 2) == 1
        for r in (1, 2, 0):
            both = [stats_in[r, n, g // 2] for n in range(2)]
            parts = [part[r, g, 0:4]] + [jnp.where(odd, x[4:8], x[0:4]) for x in both]
            top = functools.reduce(jnp.maximum, [x[0:2] for x in parts])
            lse = top + jnp.log(sum(jnp.exp(x[0:2] - top) for x in parts))
            delta = sum(jnp.exp(x[0:2] - lse) * x[2:4] for x in parts)
            for h in range(2):
                factor = jnp.exp(part[r, g, pl.ds(4 + h, 1)] - lse[h:h + 1])
                p = e_all[g, r, h] * factor
                p_low[g, h, :, r * rows:(r + 1) * rows] = p.astype(jnp.bfloat16)
                ds = p * (dp_all[g, r, h] - delta[h:h + 1])
                ds_low[g, h, :, r * rows:(r + 1) * rows] = ds.astype(jnp.bfloat16)
            columns = slice(r * rows, (r + 1) * rows)
            dq = jnp.dot(kt[g, 0], ds_low[g, 0, :, columns], preferred_element_type=jnp.float32)
            dq = dq + jnp.dot(kt[g, 1], ds_low[g, 1, :, columns], preferred_element_type=jnp.float32)
            if r == 0:
                dq_own[g] = dq
            else:
                dq_send[g, r - 1] = dq.astype(jnp.bfloat16)
                send_dq(g, r - 1).start()

    def key_gradients(g):
        columns = pl.ds(pl.multiple_of(g * COLS, COLS), COLS)
        q = qd[g, 0].reshape(3 * rows, COLS)
        do = qd[g, 1].reshape(3 * rows, COLS)
        dv = [jnp.dot(p_low[g, h], do, preferred_element_type=jnp.float32) for h in range(2)]
        dv_out[:, columns] = jnp.where(first, dv[0], dv[1]).astype(jnp.bfloat16)
        dk = [jnp.dot(ds_low[g, h], q, preferred_element_type=jnp.float32) for h in range(2)]
        dk_out[:, columns] = (jnp.where(first, dk[0], dk[1]) * scale).astype(jnp.bfloat16)

    def finish(g):
        for r in range(2):
            send_dq(g, r).wait_recv()
        dq = dq_own[g] + dq_in[g, 0].astype(jnp.float32) + dq_in[g, 1].astype(jnp.float32)
        columns = pl.ds(pl.multiple_of(g * COLS, COLS), COLS)
        dq_out[:, columns] = dq.T.astype(jnp.bfloat16)

    def step(t, carry):
        @pl.when(t < groups)
        def _():
            scores(t, 0)
            send_qd(t, 1).wait_recv()
            scores(t, 2)

        for relay, listed in RELAYS.items():
            for slot, g in enumerate(listed):
                @pl.when((place == relay) & (t == g - HOP_LEAD))
                def _():
                    hop_in(g, slot, relay).wait_recv()
                    hop_out(g, slot).start()

        @pl.when(t < groups)
        def _():
            send_qd(t, 0).wait_recv()
            scores(t, 1)

        for b in range(len(BATCHES)):
            @pl.when(t == sum(BATCHES[b]) - 1)
            def _():
                share(b)

        @pl.when(t < groups - AHEAD)
        def _():
            start_group(t + AHEAD)

        @pl.when((t >= LAG_B) & (t < groups + LAG_B))
        def _():
            gradients(t - LAG_B)

        @pl.when((t >= LAG_K) & (t < groups + LAG_K))
        def _():
            key_gradients(t - LAG_K)

        @pl.when((t >= LAG_E) & (t < groups + LAG_E))
        def _():
            finish(t - LAG_E)

        return carry

    lax.fori_loop(0, groups + max(LAG_K, LAG_E), step, 0)

    def drain(g, carry):
        for r in range(2):
            send_dq(g, r).wait_send()
        send_qd(g, 0).wait_send()

        @pl.when(jnp.logical_not(wraps & among(g, RELAYED)))
        def _():
            send_qd(g, 1).wait_send()

        return carry

    lax.fori_loop(0, groups, drain, 0)
    for relay, listed in RELAYS.items():
        for slot, g in enumerate(listed):
            @pl.when(wraps)
            def _():
                hop_in(g, slot, relay).wait_send()

            @pl.when(place == relay)
            def _():
                hop_out(g, slot).wait_send()

    for b in range(len(BATCHES)):
        for n in range(len(routes)):
            send_stats(b, n).wait_send()


def copy_kernel(*refs):
    count = len(refs) // 3
    sems = refs[-1]
    ins, outs, held = refs[:count], refs[count:2 * count], refs[2 * count:3 * count]
    loads = [pltpu.make_async_copy(ins[n], held[n], sems.at[0, n]) for n in range(count)]
    stores = [pltpu.make_async_copy(held[n], outs[n], sems.at[1, n]) for n in range(count)]
    for load in loads:
        load.start()
    for load, store in zip(loads, stores):
        load.wait()
        store.start()
    for store in stores:
        store.wait()


def local(outer_size, inner_size, queries, keys, values, d_output):
    rows, width = queries.shape
    groups = width // COLS
    block = jax.ShapeDtypeStruct((rows, width), jnp.bfloat16)
    low, wide = jnp.bfloat16, jnp.float32
    dma = pltpu.SemaphoreType.DMA
    grads = pl.pallas_call(
        functools.partial(kernel, outer_size, inner_size, groups, rows),
        out_shape=(block, block, block),
        in_specs=[pl.BlockSpec(memory_space=pl.ANY)] * 4,
        out_specs=[pl.BlockSpec(memory_space=pltpu.VMEM)] * 3,
        scratch_shapes=[
            pltpu.VMEM((groups, 2, 3, rows, COLS), low),
            pltpu.VMEM((groups, 2, rows, COLS), low),
            pltpu.VMEM((groups, 2, rows, COLS), low),
            pltpu.VMEM((groups, 2, rows, COLS), low),
            pltpu.VMEM((groups, 2, COLS, rows), low),
            pltpu.VMEM((groups, 3, 2, rows, rows), wide),
            pltpu.VMEM((groups, 3, 2, rows, rows), wide),
            pltpu.VMEM((groups, 2, rows, 3 * rows), low),
            pltpu.VMEM((groups, 2, rows, 3 * rows), low),
            pltpu.VMEM((3, groups, 8, rows), wide),
            pltpu.VMEM((3, groups // 2, 8, rows), wide),
            pltpu.VMEM((3, 2, groups // 2, 8, rows), wide),
            pltpu.VMEM((groups, COLS, rows), wide),
            pltpu.VMEM((groups, 2, COLS, rows), low),
            pltpu.VMEM((groups, 2, COLS, rows), low),
            pltpu.VMEM((3, 2, rows, COLS), low),
            dma((4, groups)),
            dma((2, groups)), dma((2, groups)),
            dma((6, len(BATCHES))), dma((6, len(BATCHES))),
            dma((2, groups)), dma((2, groups)),
            dma((groups,)), dma((3,)), dma((3,)),
        ],
        compiler_params=pltpu.CompilerParams(
            collective_id=0, has_side_effects=True, vmem_limit_bytes=58 * 2**20),
    )(queries, keys, values, d_output)
    return pl.pallas_call(
        copy_kernel,
        out_shape=(block, block, block),
        in_specs=[pl.BlockSpec(memory_space=pl.ANY)] * 3,
        out_specs=[pl.BlockSpec(memory_space=pl.ANY)] * 3,
        scratch_shapes=[pltpu.VMEM((rows, width), low)] * 3 + [dma((2, 3))],
    )(*grads)


def solution(mesh):
    spec = P(("outer", "inner"), None)
    return jax.shard_map(
        functools.partial(local, mesh.shape["outer"], mesh.shape["inner"]),
        mesh=mesh, in_specs=(spec,) * 4, out_specs=(spec,) * 3, check_vma=False)
```

```python
import functools

import jax
import jax.numpy as jnp
from jax import lax
from jax.experimental import pallas as pl
from jax.experimental.pallas import tpu as pltpu
from jax.sharding import PartitionSpec as P

HEAD = 64
COLS = 128
MESH = pl.DeviceIdType.MESH
AHEAD = 3
BATCHES = ((0,4),(4,2),(6,2))
LAG_B = 6
LAG_K = 7
LAG_E = 8
HOP_LEAD = 1
NT = (((1,), (1,)), ((), ()))
RELAYS = {2: (1, 3, 5), 4: (2, 4, 6)}
RELAYED = sum(RELAYS.values(), ())


def kernel(
    outer_size, inner_size, groups, rows,
    q_hbm, k_hbm, v_hbm, do_hbm,
    dq_out, dk_out, dv_out,
    qd, kv, km, vm, kt, e_all, dp_all, p_low, ds_low,
    part, stats, stats_in, dq_own, dq_send, dq_in, passing,
    load_sem, qd_send, qd_recv, stats_send, stats_recv,
    dq_ssem, dq_rsem, hop_send, hop_recv, pass_send,
):
    o = lax.axis_index("outer")
    i = lax.axis_index("inner")
    before = [(o, lax.rem(i + inner_size - 1, inner_size)), (lax.rem(o + outer_size - 1, outer_size), i)]
    after = [(o, lax.rem(i + 1, inner_size)), (lax.rem(o + 1, outer_size), i)]
    across = [(before[1][0], after[0][1]), (after[1][0], before[0][1])]

    def load_qd(g, which):
        src = (q_hbm, do_hbm)[which]
        return pltpu.make_async_copy(src.at[:, pl.ds(g * COLS, COLS)], qd.at[g, which, 0], load_sem.at[which, g])

    def load_kv(g, which):
        src = (k_hbm, v_hbm)[which]
        return pltpu.make_async_copy(src.at[:, pl.ds(g * COLS, COLS)], kv.at[g, which], load_sem.at[2 + which, g])

    def send_qd(g, r):
        return pltpu.make_async_remote_copy(
            qd.at[g, :, 0], qd.at[g, :, r + 1], qd_send.at[r, g], qd_recv.at[r, g],
            device_id=before[r], device_id_type=MESH)

    half = outer_size // 2
    place = lax.rem(o, half)
    base = o - place
    other = lax.rem(base + half, outer_size)
    wraps = place == 0

    def hop_in(g, slot, relay):
        return pltpu.make_async_remote_copy(
            qd.at[g, :, 0], passing.at[slot], hop_send.at[g], hop_recv.at[slot],
            device_id=(other + relay, i), device_id_type=MESH)

    def hop_out(g, slot):
        return pltpu.make_async_remote_copy(
            passing.at[slot], qd.at[g, :, 2], pass_send.at[slot], qd_recv.at[1, g],
            device_id=(base + half - 1, i), device_id_type=MESH)

    routes = (
        (0, before[0], 1, 0),
        (1, after[0], 0, 0),
        (1, across[0], 2, 1),
        (2, across[1], 1, 1),
        (0, before[1], 2, 0),
        (2, after[1], 0, 1),
    )

    def send_stats(b, n):
        r, device, there, place_there = routes[n]
        start, count = BATCHES[b]
        pairs = pl.ds(start // 2, count // 2)
        return pltpu.make_async_remote_copy(
            stats.at[r, pairs], stats_in.at[there, place_there, pairs], stats_send.at[n, b], stats_recv.at[n, b],
            device_id=device, device_id_type=MESH)

    def send_dq(g, r):
        return pltpu.make_async_remote_copy(
            dq_send.at[g, r], dq_in.at[g, r], dq_ssem.at[r, g], dq_rsem.at[r, g],
            device_id=after[r], device_id_type=MESH)

    for g in range(groups):
        for which in range(2):
            load_qd(g, which).start()
    for g in range(groups):
        for which in range(2):
            load_kv(g, which).start()

    barrier = pltpu.get_barrier_semaphore()
    for device in before + after + across:
        pl.semaphore_signal(barrier, inc=1, device_id=device, device_id_type=MESH)
    peers = {n: 6 for n in range(half)}
    for relay in RELAYS:
        @pl.when(place == relay)
        def _():
            pl.semaphore_signal(barrier, inc=1, device_id=(other, i), device_id_type=MESH)

        @pl.when(place == half - 1)
        def _():
            pl.semaphore_signal(barrier, inc=1, device_id=(base + relay, i), device_id_type=MESH)

        peers[0] += 1
        peers[relay] += 1
    for count in sorted(set(peers.values())):
        @pl.when(functools.reduce(lambda a, b: a | b, [place == n for n in range(half) if peers[n] == count]))
        def _():
            pl.semaphore_wait(barrier, count)

    def among(g, listed):
        return functools.reduce(lambda a, b: a | b, [g == n for n in listed], g < 0)

    def start_group(g):
        send_qd(g, 0).start()

        @pl.when(jnp.logical_not(wraps & among(g, RELAYED)))
        def _():
            send_qd(g, 1).start()

    for g in range(groups):
        for which in range(2):
            load_qd(g, which).wait()
        if g < AHEAD:
            start_group(jnp.int32(g))

    @pl.when(wraps)
    def _():
        for g in sorted(RELAYED):
            for relay, listed in RELAYS.items():
                if g in listed:
                    hop_in(g, listed.index(g), relay).start()

    lane = lax.broadcasted_iota(jnp.int32, (1, COLS), 1)
    first = lane < HEAD
    low = jnp.where(first, 1.0, 0.0)
    high = 1.0 - low
    scale = HEAD ** -0.5

    def prepare(g, carry):
        for which in range(2):
            load_kv(g, which).wait()
        k = kv[g, 0].astype(jnp.float32) * scale
        v = kv[g, 1].astype(jnp.float32)
        k_low, k_high = k * low, k * high
        km[g, 0] = k_low.astype(jnp.bfloat16)
        km[g, 1] = k_high.astype(jnp.bfloat16)
        vm[g, 0] = (v * low).astype(jnp.bfloat16)
        vm[g, 1] = (v * high).astype(jnp.bfloat16)
        kt[g, 0] = k_low.T.astype(jnp.bfloat16)
        kt[g, 1] = k_high.T.astype(jnp.bfloat16)
        return carry

    lax.fori_loop(0, groups, prepare, 0)

    def scores(g, r):
        q = qd[g, 0, r]
        do = qd[g, 1, r]
        for h in range(2):
            s = lax.dot_general(km[g, h], q, NT, preferred_element_type=jnp.float32)
            dp = lax.dot_general(vm[g, h], do, NT, preferred_element_type=jnp.float32)
            top = jnp.max(s, axis=0, keepdims=True)
            e = jnp.exp(s - top)
            e_all[g, r, h] = e
            dp_all[g, r, h] = dp
            norm = jnp.sum(e, axis=0, keepdims=True)
            part[r, g, pl.ds(h, 1)] = top + jnp.log(norm)
            part[r, g, pl.ds(2 + h, 1)] = jnp.sum(e * dp, axis=0, keepdims=True) / norm
            part[r, g, pl.ds(4 + h, 1)] = top

    def share(b):
        start, count = BATCHES[b]
        for r in range(3):
            for g in range(start, start + count, 2):
                stats[r, g // 2, 0:4] = part[r, g, 0:4]
                stats[r, g // 2, 4:8] = part[r, g + 1, 0:4]
        for n in range(len(routes)):
            send_stats(b, n).start()

    def gradients(g):
        for b in range(len(BATCHES)):
            @pl.when(g == BATCHES[b][0])
            def _():
                for n in range(len(routes)):
                    send_stats(b, n).wait_recv()

        odd = lax.rem(g, 2) == 1
        for r in (1, 2, 0):
            both = [stats_in[r, n, g // 2] for n in range(2)]
            parts = [part[r, g, 0:4]] + [jnp.where(odd, x[4:8], x[0:4]) for x in both]
            top = functools.reduce(jnp.maximum, [x[0:2] for x in parts])
            lse = top + jnp.log(sum(jnp.exp(x[0:2] - top) for x in parts))
            delta = sum(jnp.exp(x[0:2] - lse) * x[2:4] for x in parts)
            for h in range(2):
                factor = jnp.exp(part[r, g, pl.ds(4 + h, 1)] - lse[h:h + 1])
                p = e_all[g, r, h] * factor
                p_low[g, h, :, r * rows:(r + 1) * rows] = p.astype(jnp.bfloat16)
                ds = p * (dp_all[g, r, h] - delta[h:h + 1])
                ds_low[g, h, :, r * rows:(r + 1) * rows] = ds.astype(jnp.bfloat16)
            columns = slice(r * rows, (r + 1) * rows)
            dq = jnp.dot(kt[g, 0], ds_low[g, 0, :, columns], preferred_element_type=jnp.float32)
            dq = dq + jnp.dot(kt[g, 1], ds_low[g, 1, :, columns], preferred_element_type=jnp.float32)
            if r == 0:
                dq_own[g] = dq
            else:
                dq_send[g, r - 1] = dq.astype(jnp.bfloat16)
                send_dq(g, r - 1).start()

    def key_gradients(g):
        columns = pl.ds(pl.multiple_of(g * COLS, COLS), COLS)
        q = qd[g, 0].reshape(3 * rows, COLS)
        do = qd[g, 1].reshape(3 * rows, COLS)
        dv = [jnp.dot(p_low[g, h], do, preferred_element_type=jnp.float32) for h in range(2)]
        dv_out[:, columns] = jnp.where(first, dv[0], dv[1]).astype(jnp.bfloat16)
        dk = [jnp.dot(ds_low[g, h], q, preferred_element_type=jnp.float32) for h in range(2)]
        dk_out[:, columns] = (jnp.where(first, dk[0], dk[1]) * scale).astype(jnp.bfloat16)

    def finish(g):
        for r in range(2):
            send_dq(g, r).wait_recv()
        dq = dq_own[g] + dq_in[g, 0].astype(jnp.float32) + dq_in[g, 1].astype(jnp.float32)
        columns = pl.ds(pl.multiple_of(g * COLS, COLS), COLS)
        dq_out[:, columns] = dq.T.astype(jnp.bfloat16)

    def step(t, carry):
        @pl.when(t < groups)
        def _():
            scores(t, 0)
            send_qd(t, 1).wait_recv()
            scores(t, 2)

        for relay, listed in RELAYS.items():
            for slot, g in enumerate(listed):
                @pl.when((place == relay) & (t == g - HOP_LEAD))
                def _():
                    hop_in(g, slot, relay).wait_recv()
                    hop_out(g, slot).start()

        @pl.when(t < groups)
        def _():
            send_qd(t, 0).wait_recv()
            scores(t, 1)

        for b in range(len(BATCHES)):
            @pl.when(t == sum(BATCHES[b]) - 1)
            def _():
                share(b)

        @pl.when(t < groups - AHEAD)
        def _():
            start_group(t + AHEAD)

        @pl.when((t >= LAG_B) & (t < groups + LAG_B))
        def _():
            gradients(t - LAG_B)

        @pl.when((t >= LAG_K) & (t < groups + LAG_K))
        def _():
            key_gradients(t - LAG_K)

        @pl.when((t >= LAG_E) & (t < groups + LAG_E))
        def _():
            finish(t - LAG_E)

        return carry

    lax.fori_loop(0, groups + max(LAG_K, LAG_E), step, 0)

    def drain(g, carry):
        for r in range(2):
            send_dq(g, r).wait_send()
        send_qd(g, 0).wait_send()

        @pl.when(jnp.logical_not(wraps & among(g, RELAYED)))
        def _():
            send_qd(g, 1).wait_send()

        return carry

    lax.fori_loop(0, groups, drain, 0)
    for relay, listed in RELAYS.items():
        for slot, g in enumerate(listed):
            @pl.when(wraps)
            def _():
                hop_in(g, slot, relay).wait_send()

            @pl.when(place == relay)
            def _():
                hop_out(g, slot).wait_send()

    for b in range(len(BATCHES)):
        for n in range(len(routes)):
            send_stats(b, n).wait_send()


def copy_kernel(*refs):
    count = len(refs) // 3
    sems = refs[-1]
    ins, outs, held = refs[:count], refs[count:2 * count], refs[2 * count:3 * count]
    loads = [pltpu.make_async_copy(ins[n], held[n], sems.at[0, n]) for n in range(count)]
    stores = [pltpu.make_async_copy(held[n], outs[n], sems.at[1, n]) for n in range(count)]
    for load in loads:
        load.start()
    for load, store in zip(loads, stores):
        load.wait()
        store.start()
    for store in stores:
        store.wait()


def local(outer_size, inner_size, queries, keys, values, d_output):
    rows, width = queries.shape
    groups = width // COLS
    block = jax.ShapeDtypeStruct((rows, width), jnp.bfloat16)
    low, wide = jnp.bfloat16, jnp.float32
    dma = pltpu.SemaphoreType.DMA
    grads = pl.pallas_call(
        functools.partial(kernel, outer_size, inner_size, groups, rows),
        out_shape=(block, block, block),
        in_specs=[pl.BlockSpec(memory_space=pl.ANY)] * 4,
        out_specs=[pl.BlockSpec(memory_space=pltpu.VMEM)] * 3,
        scratch_shapes=[
            pltpu.VMEM((groups, 2, 3, rows, COLS), low),
            pltpu.VMEM((groups, 2, rows, COLS), low),
            pltpu.VMEM((groups, 2, rows, COLS), low),
            pltpu.VMEM((groups, 2, rows, COLS), low),
            pltpu.VMEM((groups, 2, COLS, rows), low),
            pltpu.VMEM((groups, 3, 2, rows, rows), wide),
            pltpu.VMEM((groups, 3, 2, rows, rows), wide),
            pltpu.VMEM((groups, 2, rows, 3 * rows), low),
            pltpu.VMEM((groups, 2, rows, 3 * rows), low),
            pltpu.VMEM((3, groups, 8, rows), wide),
            pltpu.VMEM((3, groups // 2, 8, rows), wide),
            pltpu.VMEM((3, 2, groups // 2, 8, rows), wide),
            pltpu.VMEM((groups, COLS, rows), wide),
            pltpu.VMEM((groups, 2, COLS, rows), low),
            pltpu.VMEM((groups, 2, COLS, rows), low),
            pltpu.VMEM((3, 2, rows, COLS), low),
            dma((4, groups)),
            dma((2, groups)), dma((2, groups)),
            dma((6, len(BATCHES))), dma((6, len(BATCHES))),
            dma((2, groups)), dma((2, groups)),
            dma((groups,)), dma((3,)), dma((3,)),
        ],
        compiler_params=pltpu.CompilerParams(
            collective_id=0, has_side_effects=True, vmem_limit_bytes=58 * 2**20),
    )(queries, keys, values, d_output)
    return pl.pallas_call(
        copy_kernel,
        out_shape=(block, block, block),
        in_specs=[pl.BlockSpec(memory_space=pl.ANY)] * 3,
        out_specs=[pl.BlockSpec(memory_space=pl.ANY)] * 3,
        scratch_shapes=[pltpu.VMEM((rows, width), low)] * 3 + [dma((2, 3))],
    )(*grads)


def solution(mesh):
    spec = P(("outer", "inner"), None)
    return jax.shard_map(
        functools.partial(local, mesh.shape["outer"], mesh.shape["inner"]),
        mesh=mesh, in_specs=(spec,) * 4, out_specs=(spec,) * 3, check_vma=False)
```

```python
import functools

import jax
import jax.numpy as jnp
from jax import lax
from jax.experimental import pallas as pl
from jax.experimental.pallas import tpu as pltpu
from jax.sharding import PartitionSpec as P

HEAD = 64
COLS = 128
MESH = pl.DeviceIdType.MESH
AHEAD = 3
BATCHES = ((0,4),(4,2),(6,2))
LAG_B = 6
LAG_K = 7
LAG_E = 8
HOP_LEAD = 1
NT = (((1,), (1,)), ((), ()))
RELAYS = {2: (1, 3, 5), 4: (2, 4, 6)}
RELAYED = sum(RELAYS.values(), ())


def kernel(
    outer_size, inner_size, groups, rows,
    q_hbm, k_hbm, v_hbm, do_hbm,
    dq_out, dk_out, dv_out,
    qd, kv, km, vm, kt, e_all, dp_all, p_low, ds_low,
    part, stats, stats_in, dq_own, dq_send, dq_in, passing,
    dq_held, dk_held, dv_held, store_sem,
    load_sem, qd_send, qd_recv, stats_send, stats_recv,
    dq_ssem, dq_rsem, hop_send, hop_recv, pass_send,
):
    o = lax.axis_index("outer")
    i = lax.axis_index("inner")
    before = [(o, lax.rem(i + inner_size - 1, inner_size)), (lax.rem(o + outer_size - 1, outer_size), i)]
    after = [(o, lax.rem(i + 1, inner_size)), (lax.rem(o + 1, outer_size), i)]
    across = [(before[1][0], after[0][1]), (after[1][0], before[0][1])]

    def load_qd(g, which):
        src = (q_hbm, do_hbm)[which]
        return pltpu.make_async_copy(src.at[:, pl.ds(g * COLS, COLS)], qd.at[g, which, 0], load_sem.at[which, g])

    def load_kv(g, which):
        src = (k_hbm, v_hbm)[which]
        return pltpu.make_async_copy(src.at[:, pl.ds(g * COLS, COLS)], kv.at[g, which], load_sem.at[2 + which, g])

    def store(g, which):
        src = (dq_held, dk_held, dv_held)[which]
        dst = (dq_out, dk_out, dv_out)[which]
        columns = pl.ds(pl.multiple_of(g * COLS, COLS), COLS)
        return pltpu.make_async_copy(src.at[g], dst.at[:, columns], store_sem.at[which, g])

    def send_qd(g, r):
        return pltpu.make_async_remote_copy(
            qd.at[g, :, 0], qd.at[g, :, r + 1], qd_send.at[r, g], qd_recv.at[r, g],
            device_id=before[r], device_id_type=MESH)

    half = outer_size // 2
    place = lax.rem(o, half)
    base = o - place
    other = lax.rem(base + half, outer_size)
    wraps = place == 0

    def hop_in(g, slot, relay):
        return pltpu.make_async_remote_copy(
            qd.at[g, :, 0], passing.at[slot], hop_send.at[g], hop_recv.at[slot],
            device_id=(other + relay, i), device_id_type=MESH)

    def hop_out(g, slot):
        return pltpu.make_async_remote_copy(
            passing.at[slot], qd.at[g, :, 2], pass_send.at[slot], qd_recv.at[1, g],
            device_id=(base + half - 1, i), device_id_type=MESH)

    routes = (
        (0, before[0], 1, 0),
        (1, after[0], 0, 0),
        (1, across[0], 2, 1),
        (2, across[1], 1, 1),
        (0, before[1], 2, 0),
        (2, after[1], 0, 1),
    )

    def send_stats(b, n):
        r, device, there, place_there = routes[n]
        start, count = BATCHES[b]
        pairs = pl.ds(start // 2, count // 2)
        return pltpu.make_async_remote_copy(
            stats.at[r, pairs], stats_in.at[there, place_there, pairs], stats_send.at[n, b], stats_recv.at[n, b],
            device_id=device, device_id_type=MESH)

    def send_dq(g, r):
        return pltpu.make_async_remote_copy(
            dq_send.at[g, r], dq_in.at[g, r], dq_ssem.at[r, g], dq_rsem.at[r, g],
            device_id=after[r], device_id_type=MESH)

    barrier = pltpu.get_barrier_semaphore()
    for device in before + after + across:
        pl.semaphore_signal(barrier, inc=1, device_id=device, device_id_type=MESH)
    peers = {n: 6 for n in range(half)}
    for relay in RELAYS:
        @pl.when(place == relay)
        def _():
            pl.semaphore_signal(barrier, inc=1, device_id=(other, i), device_id_type=MESH)

        @pl.when(place == half - 1)
        def _():
            pl.semaphore_signal(barrier, inc=1, device_id=(base + relay, i), device_id_type=MESH)

        peers[0] += 1
        peers[relay] += 1
    for g in range(groups):
        for which in range(2):
            load_qd(g, which).start()
    for g in range(groups):
        for which in range(2):
            load_kv(g, which).start()

    for count in sorted(set(peers.values())):
        @pl.when(functools.reduce(lambda a, b: a | b, [place == n for n in range(half) if peers[n] == count]))
        def _():
            pl.semaphore_wait(barrier, count)

    def among(g, listed):
        return functools.reduce(lambda a, b: a | b, [g == n for n in listed], g < 0)

    def start_group(g):
        send_qd(g, 0).start()

        @pl.when(jnp.logical_not(wraps & among(g, RELAYED)))
        def _():
            send_qd(g, 1).start()

    for g in range(groups):
        for which in range(2):
            load_qd(g, which).wait()
        if g < AHEAD:
            start_group(jnp.int32(g))

    @pl.when(wraps)
    def _():
        for g in sorted(RELAYED):
            for relay, listed in RELAYS.items():
                if g in listed:
                    hop_in(g, listed.index(g), relay).start()

    lane = lax.broadcasted_iota(jnp.int32, (1, COLS), 1)
    first = lane < HEAD
    low = jnp.where(first, 1.0, 0.0)
    high = 1.0 - low
    scale = HEAD ** -0.5

    def prepare(g, carry):
        for which in range(2):
            load_kv(g, which).wait()
        k = kv[g, 0].astype(jnp.float32) * scale
        v = kv[g, 1].astype(jnp.float32)
        k_low, k_high = k * low, k * high
        km[g, 0] = k_low.astype(jnp.bfloat16)
        km[g, 1] = k_high.astype(jnp.bfloat16)
        vm[g, 0] = (v * low).astype(jnp.bfloat16)
        vm[g, 1] = (v * high).astype(jnp.bfloat16)
        kt[g, 0] = k_low.T.astype(jnp.bfloat16)
        kt[g, 1] = k_high.T.astype(jnp.bfloat16)
        return carry

    lax.fori_loop(0, groups, prepare, 0)

    def scores(g, r):
        q = qd[g, 0, r]
        do = qd[g, 1, r]
        for h in range(2):
            s = lax.dot_general(km[g, h], q, NT, preferred_element_type=jnp.float32)
            dp = lax.dot_general(vm[g, h], do, NT, preferred_element_type=jnp.float32)
            top = jnp.max(s, axis=0, keepdims=True)
            e = jnp.exp(s - top)
            e_all[g, r, h] = e
            dp_all[g, r, h] = dp
            norm = jnp.sum(e, axis=0, keepdims=True)
            part[r, g, pl.ds(h, 1)] = top + jnp.log(norm)
            part[r, g, pl.ds(2 + h, 1)] = jnp.sum(e * dp, axis=0, keepdims=True) / norm
            part[r, g, pl.ds(4 + h, 1)] = top

    def share(b):
        start, count = BATCHES[b]
        for r in range(3):
            for g in range(start, start + count, 2):
                stats[r, g // 2, 0:4] = part[r, g, 0:4]
                stats[r, g // 2, 4:8] = part[r, g + 1, 0:4]
        for n in range(len(routes)):
            send_stats(b, n).start()

    def gradients(g):
        for b in range(len(BATCHES)):
            @pl.when(g == BATCHES[b][0])
            def _():
                for n in range(len(routes)):
                    send_stats(b, n).wait_recv()

        odd = lax.rem(g, 2) == 1
        for r in (1, 2, 0):
            both = [stats_in[r, n, g // 2] for n in range(2)]
            parts = [part[r, g, 0:4]] + [jnp.where(odd, x[4:8], x[0:4]) for x in both]
            top = functools.reduce(jnp.maximum, [x[0:2] for x in parts])
            lse = top + jnp.log(sum(jnp.exp(x[0:2] - top) for x in parts))
            delta = sum(jnp.exp(x[0:2] - lse) * x[2:4] for x in parts)
            for h in range(2):
                factor = jnp.exp(part[r, g, pl.ds(4 + h, 1)] - lse[h:h + 1])
                p = e_all[g, r, h] * factor
                p_low[g, h, :, r * rows:(r + 1) * rows] = p.astype(jnp.bfloat16)
                ds = p * (dp_all[g, r, h] - delta[h:h + 1])
                ds_low[g, h, :, r * rows:(r + 1) * rows] = ds.astype(jnp.bfloat16)
            columns = slice(r * rows, (r + 1) * rows)
            dq = jnp.dot(kt[g, 0], ds_low[g, 0, :, columns], preferred_element_type=jnp.float32)
            dq = dq + jnp.dot(kt[g, 1], ds_low[g, 1, :, columns], preferred_element_type=jnp.float32)
            if r == 0:
                dq_own[g] = dq
            else:
                dq_send[g, r - 1] = dq.astype(jnp.bfloat16)
                send_dq(g, r - 1).start()

    def key_gradients(g):
        q = qd[g, 0].reshape(3 * rows, COLS)
        do = qd[g, 1].reshape(3 * rows, COLS)
        dv = [jnp.dot(p_low[g, h], do, preferred_element_type=jnp.float32) for h in range(2)]
        dv_held[g] = jnp.where(first, dv[0], dv[1]).astype(jnp.bfloat16)
        dk = [jnp.dot(ds_low[g, h], q, preferred_element_type=jnp.float32) for h in range(2)]
        dk_held[g] = (jnp.where(first, dk[0], dk[1]) * scale).astype(jnp.bfloat16)
        store(g, 1).start()
        store(g, 2).start()

    def finish(g):
        for r in range(2):
            send_dq(g, r).wait_recv()
        dq = dq_own[g] + dq_in[g, 0].astype(jnp.float32) + dq_in[g, 1].astype(jnp.float32)
        dq_held[g] = dq.T.astype(jnp.bfloat16)
        store(g, 0).start()

    def step(t, carry):
        @pl.when(t < groups - AHEAD)
        def _():
            start_group(t + AHEAD)

        @pl.when(t < groups)
        def _():
            scores(t, 0)
            send_qd(t, 1).wait_recv()
            scores(t, 2)

        for relay, listed in RELAYS.items():
            for slot, g in enumerate(listed):
                @pl.when((place == relay) & (t == g - HOP_LEAD))
                def _():
                    hop_in(g, slot, relay).wait_recv()
                    hop_out(g, slot).start()

        @pl.when(t < groups)
        def _():
            send_qd(t, 0).wait_recv()
            scores(t, 1)

        for b in range(len(BATCHES)):
            @pl.when(t == sum(BATCHES[b]) - 1)
            def _():
                share(b)

        @pl.when((t >= LAG_B) & (t < groups + LAG_B))
        def _():
            gradients(t - LAG_B)

        @pl.when((t >= LAG_K) & (t < groups + LAG_K))
        def _():
            key_gradients(t - LAG_K)

        @pl.when((t >= LAG_E) & (t < groups + LAG_E))
        def _():
            finish(t - LAG_E)

        return carry

    lax.fori_loop(0, groups + max(LAG_K, LAG_E), step, 0)

    def drain(g, carry):
        for r in range(2):
            send_dq(g, r).wait_send()
        for which in range(3):
            store(g, which).wait()
        send_qd(g, 0).wait_send()

        @pl.when(jnp.logical_not(wraps & among(g, RELAYED)))
        def _():
            send_qd(g, 1).wait_send()

        return carry

    lax.fori_loop(0, groups, drain, 0)
    for relay, listed in RELAYS.items():
        for slot, g in enumerate(listed):
            @pl.when(wraps)
            def _():
                hop_in(g, slot, relay).wait_send()

            @pl.when(place == relay)
            def _():
                hop_out(g, slot).wait_send()

    for b in range(len(BATCHES)):
        for n in range(len(routes)):
            send_stats(b, n).wait_send()


def copy_kernel(*refs):
    count = len(refs) // 3
    sems = refs[-1]
    ins, outs, held = refs[:count], refs[count:2 * count], refs[2 * count:3 * count]
    loads = [pltpu.make_async_copy(ins[n], held[n], sems.at[0, n]) for n in range(count)]
    stores = [pltpu.make_async_copy(held[n], outs[n], sems.at[1, n]) for n in range(count)]
    for load in loads:
        load.start()
    for load, store in zip(loads, stores):
        load.wait()
        store.start()
    for store in stores:
        store.wait()


def local(outer_size, inner_size, queries, keys, values, d_output):
    rows, width = queries.shape
    groups = width // COLS
    block = jax.ShapeDtypeStruct((rows, width), jnp.bfloat16)
    low, wide = jnp.bfloat16, jnp.float32
    dma = pltpu.SemaphoreType.DMA
    grads = pl.pallas_call(
        functools.partial(kernel, outer_size, inner_size, groups, rows),
        out_shape=(block, block, block),
        in_specs=[pl.BlockSpec(memory_space=pl.ANY)] * 4,
        out_specs=[pl.BlockSpec(memory_space=pl.ANY)] * 3,
        scratch_shapes=[
            pltpu.VMEM((groups, 2, 3, rows, COLS), low),
            pltpu.VMEM((groups, 2, rows, COLS), low),
            pltpu.VMEM((groups, 2, rows, COLS), low),
            pltpu.VMEM((groups, 2, rows, COLS), low),
            pltpu.VMEM((groups, 2, COLS, rows), low),
            pltpu.VMEM((groups, 3, 2, rows, rows), wide),
            pltpu.VMEM((groups, 3, 2, rows, rows), wide),
            pltpu.VMEM((groups, 2, rows, 3 * rows), low),
            pltpu.VMEM((groups, 2, rows, 3 * rows), low),
            pltpu.VMEM((3, groups, 8, rows), wide),
            pltpu.VMEM((3, groups // 2, 8, rows), wide),
            pltpu.VMEM((3, 2, groups // 2, 8, rows), wide),
            pltpu.VMEM((groups, COLS, rows), wide),
            pltpu.VMEM((groups, 2, COLS, rows), low),
            pltpu.VMEM((groups, 2, COLS, rows), low),
            pltpu.VMEM((3, 2, rows, COLS), low),
            pltpu.VMEM((groups, rows, COLS), low),
            pltpu.VMEM((groups, rows, COLS), low),
            pltpu.VMEM((groups, rows, COLS), low),
            dma((3, groups)),
            dma((4, groups)),
            dma((2, groups)), dma((2, groups)),
            dma((6, len(BATCHES))), dma((6, len(BATCHES))),
            dma((2, groups)), dma((2, groups)),
            dma((groups,)), dma((3,)), dma((3,)),
        ],
        compiler_params=pltpu.CompilerParams(
            collective_id=0, has_side_effects=True, vmem_limit_bytes=58 * 2**20),
    )(queries, keys, values, d_output)
    return pl.pallas_call(
        copy_kernel,
        out_shape=(block, block, block),
        in_specs=[pl.BlockSpec(memory_space=pl.ANY)] * 3,
        out_specs=[pl.BlockSpec(memory_space=pl.ANY)] * 3,
        scratch_shapes=[pltpu.VMEM((rows, width), low)] * 3 + [dma((2, 3))],
    )(*grads)


def solution(mesh):
    spec = P(("outer", "inner"), None)
    return jax.shard_map(
        functools.partial(local, mesh.shape["outer"], mesh.shape["inner"]),
        mesh=mesh, in_specs=(spec,) * 4, out_specs=(spec,) * 3, check_vma=False)
```

```python
import functools

import jax
import jax.numpy as jnp
from jax import lax
from jax.experimental import pallas as pl
from jax.experimental.pallas import tpu as pltpu
from jax.sharding import PartitionSpec as P

HEAD = 64
COLS = 128
MESH = pl.DeviceIdType.MESH
AHEAD = 4
BATCHES = ((0,2),(2,2),(4,2),(6,2))
LAG_B = 6
LAG_K = 7
LAG_E = 8
HOP_LEAD = 1
NT = (((1,), (1,)), ((), ()))
RELAYS = {2: (1, 3, 5), 4: (2, 4, 6)}
RELAYED = sum(RELAYS.values(), ())


def kernel(
    outer_size, inner_size, groups, rows,
    q_hbm, k_hbm, v_hbm, do_hbm,
    dq_out, dk_out, dv_out,
    qd, kv, km, vm, kt, e_all, dp_all, p_low, ds_low,
    part, stats, stats_in, dq_own, dq_send, dq_in, passing,
    dq_held, dk_held, dv_held, store_sem,
    load_sem, qd_send, qd_recv, stats_send, stats_recv,
    dq_ssem, dq_rsem, hop_send, hop_recv, pass_send,
):
    o = lax.axis_index("outer")
    i = lax.axis_index("inner")
    before = [(o, lax.rem(i + inner_size - 1, inner_size)), (lax.rem(o + outer_size - 1, outer_size), i)]
    after = [(o, lax.rem(i + 1, inner_size)), (lax.rem(o + 1, outer_size), i)]
    across = [(before[1][0], after[0][1]), (after[1][0], before[0][1])]

    def load_qd(g, which):
        src = (q_hbm, do_hbm)[which]
        return pltpu.make_async_copy(src.at[:, pl.ds(g * COLS, COLS)], qd.at[g, which, 0], load_sem.at[which, g])

    def load_kv(g, which):
        src = (k_hbm, v_hbm)[which]
        return pltpu.make_async_copy(src.at[:, pl.ds(g * COLS, COLS)], kv.at[g, which], load_sem.at[2 + which, g])

    def store(g, which):
        src = (dq_held, dk_held, dv_held)[which]
        dst = (dq_out, dk_out, dv_out)[which]
        columns = pl.ds(pl.multiple_of(g * COLS, COLS), COLS)
        return pltpu.make_async_copy(src.at[g], dst.at[:, columns], store_sem.at[which, g])

    def send_qd(g, r):
        return pltpu.make_async_remote_copy(
            qd.at[g, :, 0], qd.at[g, :, r + 1], qd_send.at[r, g], qd_recv.at[r, g],
            device_id=before[r], device_id_type=MESH)

    half = outer_size // 2
    place = lax.rem(o, half)
    base = o - place
    other = lax.rem(base + half, outer_size)
    wraps = place == 0

    def hop_in(g, slot, relay):
        return pltpu.make_async_remote_copy(
            qd.at[g, :, 0], passing.at[slot], hop_send.at[g], hop_recv.at[slot],
            device_id=(other + relay, i), device_id_type=MESH)

    def hop_out(g, slot):
        return pltpu.make_async_remote_copy(
            passing.at[slot], qd.at[g, :, 2], pass_send.at[slot], qd_recv.at[1, g],
            device_id=(base + half - 1, i), device_id_type=MESH)

    routes = (
        (0, before[0], 1, 0),
        (1, after[0], 0, 0),
        (1, across[0], 2, 1),
        (2, across[1], 1, 1),
        (0, before[1], 2, 0),
        (2, after[1], 0, 1),
    )

    def send_stats(b, n):
        r, device, there, place_there = routes[n]
        start, count = BATCHES[b]
        pairs = pl.ds(start // 2, count // 2)
        return pltpu.make_async_remote_copy(
            stats.at[r, pairs], stats_in.at[there, place_there, pairs], stats_send.at[n, b], stats_recv.at[n, b],
            device_id=device, device_id_type=MESH)

    def send_dq(g, r):
        return pltpu.make_async_remote_copy(
            dq_send.at[g, r], dq_in.at[g, r], dq_ssem.at[r, g], dq_rsem.at[r, g],
            device_id=after[r], device_id_type=MESH)

    barrier = pltpu.get_barrier_semaphore()
    for device in before + after + across:
        pl.semaphore_signal(barrier, inc=1, device_id=device, device_id_type=MESH)
    peers = {n: 6 for n in range(half)}
    for relay in RELAYS:
        @pl.when(place == relay)
        def _():
            pl.semaphore_signal(barrier, inc=1, device_id=(other, i), device_id_type=MESH)

        @pl.when(place == half - 1)
        def _():
            pl.semaphore_signal(barrier, inc=1, device_id=(base + relay, i), device_id_type=MESH)

        peers[0] += 1
        peers[relay] += 1
    for g in range(groups):
        for which in range(2):
            load_qd(g, which).start()
    for g in range(groups):
        for which in range(2):
            load_kv(g, which).start()

    for count in sorted(set(peers.values())):
        @pl.when(functools.reduce(lambda a, b: a | b, [place == n for n in range(half) if peers[n] == count]))
        def _():
            pl.semaphore_wait(barrier, count)

    def among(g, listed):
        return functools.reduce(lambda a, b: a | b, [g == n for n in listed], g < 0)

    def start_group(g):
        send_qd(g, 0).start()

        @pl.when(jnp.logical_not(wraps & among(g, RELAYED)))
        def _():
            send_qd(g, 1).start()

    for g in range(groups):
        for which in range(2):
            load_qd(g, which).wait()
        if g < AHEAD:
            start_group(jnp.int32(g))

    @pl.when(wraps)
    def _():
        for g in sorted(RELAYED):
            for relay, listed in RELAYS.items():
                if g in listed:
                    hop_in(g, listed.index(g), relay).start()

    lane = lax.broadcasted_iota(jnp.int32, (1, COLS), 1)
    first = lane < HEAD
    low = jnp.where(first, 1.0, 0.0)
    high = 1.0 - low
    scale = HEAD ** -0.5

    def prepare(g, carry):
        for which in range(2):
            load_kv(g, which).wait()
        k = kv[g, 0].astype(jnp.float32) * scale
        v = kv[g, 1].astype(jnp.float32)
        k_low, k_high = k * low, k * high
        km[g, 0] = k_low.astype(jnp.bfloat16)
        km[g, 1] = k_high.astype(jnp.bfloat16)
        vm[g, 0] = (v * low).astype(jnp.bfloat16)
        vm[g, 1] = (v * high).astype(jnp.bfloat16)
        kt[g, 0] = k_low.T.astype(jnp.bfloat16)
        kt[g, 1] = k_high.T.astype(jnp.bfloat16)
        return carry

    lax.fori_loop(0, groups, prepare, 0)

    def scores(g, r):
        q = qd[g, 0, r]
        do = qd[g, 1, r]
        for h in range(2):
            s = lax.dot_general(km[g, h], q, NT, preferred_element_type=jnp.float32)
            dp = lax.dot_general(vm[g, h], do, NT, preferred_element_type=jnp.float32)
            top = jnp.max(s, axis=0, keepdims=True)
            e = jnp.exp(s - top)
            e_all[g, r, h] = e
            dp_all[g, r, h] = dp
            norm = jnp.sum(e, axis=0, keepdims=True)
            part[r, g, pl.ds(h, 1)] = top + jnp.log(norm)
            part[r, g, pl.ds(2 + h, 1)] = jnp.sum(e * dp, axis=0, keepdims=True) / norm
            part[r, g, pl.ds(4 + h, 1)] = top

    def share(b):
        start, count = BATCHES[b]
        for r in range(3):
            for g in range(start, start + count, 2):
                stats[r, g // 2, 0:4] = part[r, g, 0:4]
                stats[r, g // 2, 4:8] = part[r, g + 1, 0:4]
        for n in range(len(routes)):
            send_stats(b, n).start()

    def gradients(g):
        for b in range(len(BATCHES)):
            @pl.when(g == BATCHES[b][0])
            def _():
                for n in range(len(routes)):
                    send_stats(b, n).wait_recv()

        odd = lax.rem(g, 2) == 1
        for r in (1, 2, 0):
            both = [stats_in[r, n, g // 2] for n in range(2)]
            parts = [part[r, g, 0:4]] + [jnp.where(odd, x[4:8], x[0:4]) for x in both]
            top = functools.reduce(jnp.maximum, [x[0:2] for x in parts])
            lse = top + jnp.log(sum(jnp.exp(x[0:2] - top) for x in parts))
            delta = sum(jnp.exp(x[0:2] - lse) * x[2:4] for x in parts)
            for h in range(2):
                factor = jnp.exp(part[r, g, pl.ds(4 + h, 1)] - lse[h:h + 1])
                p = e_all[g, r, h] * factor
                p_low[g, h, :, r * rows:(r + 1) * rows] = p.astype(jnp.bfloat16)
                ds = p * (dp_all[g, r, h] - delta[h:h + 1])
                ds_low[g, h, :, r * rows:(r + 1) * rows] = ds.astype(jnp.bfloat16)
            columns = slice(r * rows, (r + 1) * rows)
            dq = jnp.dot(kt[g, 0], ds_low[g, 0, :, columns], preferred_element_type=jnp.float32)
            dq = dq + jnp.dot(kt[g, 1], ds_low[g, 1, :, columns], preferred_element_type=jnp.float32)
            if r == 0:
                dq_own[g] = dq
            else:
                dq_send[g, r - 1] = dq.astype(jnp.bfloat16)
                send_dq(g, r - 1).start()

    def key_gradients(g):
        q = qd[g, 0].reshape(3 * rows, COLS)
        do = qd[g, 1].reshape(3 * rows, COLS)
        dv = [jnp.dot(p_low[g, h], do, preferred_element_type=jnp.float32) for h in range(2)]
        dv_held[g] = jnp.where(first, dv[0], dv[1]).astype(jnp.bfloat16)
        dk = [jnp.dot(ds_low[g, h], q, preferred_element_type=jnp.float32) for h in range(2)]
        dk_held[g] = (jnp.where(first, dk[0], dk[1]) * scale).astype(jnp.bfloat16)
        store(g, 1).start()
        store(g, 2).start()

    def finish(g):
        for r in range(2):
            send_dq(g, r).wait_recv()
        dq = dq_own[g] + dq_in[g, 0].astype(jnp.float32) + dq_in[g, 1].astype(jnp.float32)
        dq_held[g] = dq.T.astype(jnp.bfloat16)
        store(g, 0).start()

    def step(t, carry):
        @pl.when(t < groups - AHEAD)
        def _():
            start_group(t + AHEAD)

        @pl.when(t < groups)
        def _():
            scores(t, 0)
            send_qd(t, 1).wait_recv()
            scores(t, 2)

        for relay, listed in RELAYS.items():
            for slot, g in enumerate(listed):
                @pl.when((place == relay) & (t == g - HOP_LEAD))
                def _():
                    hop_in(g, slot, relay).wait_recv()
                    hop_out(g, slot).start()

        @pl.when(t < groups)
        def _():
            send_qd(t, 0).wait_recv()
            scores(t, 1)

        for b in range(len(BATCHES)):
            @pl.when(t == sum(BATCHES[b]) - 1)
            def _():
                share(b)

        @pl.when((t >= LAG_B) & (t < groups + LAG_B))
        def _():
            gradients(t - LAG_B)

        @pl.when((t >= LAG_K) & (t < groups + LAG_K))
        def _():
            key_gradients(t - LAG_K)

        @pl.when((t >= LAG_E) & (t < groups + LAG_E))
        def _():
            finish(t - LAG_E)

        return carry

    lax.fori_loop(0, groups + max(LAG_K, LAG_E), step, 0)

    def drain(g, carry):
        for r in range(2):
            send_dq(g, r).wait_send()
        for which in range(3):
            store(g, which).wait()
        send_qd(g, 0).wait_send()

        @pl.when(jnp.logical_not(wraps & among(g, RELAYED)))
        def _():
            send_qd(g, 1).wait_send()

        return carry

    lax.fori_loop(0, groups, drain, 0)
    for relay, listed in RELAYS.items():
        for slot, g in enumerate(listed):
            @pl.when(wraps)
            def _():
                hop_in(g, slot, relay).wait_send()

            @pl.when(place == relay)
            def _():
                hop_out(g, slot).wait_send()

    for b in range(len(BATCHES)):
        for n in range(len(routes)):
            send_stats(b, n).wait_send()


def copy_kernel(*refs):
    count = len(refs) // 3
    sems = refs[-1]
    ins, outs, held = refs[:count], refs[count:2 * count], refs[2 * count:3 * count]
    loads = [pltpu.make_async_copy(ins[n], held[n], sems.at[0, n]) for n in range(count)]
    stores = [pltpu.make_async_copy(held[n], outs[n], sems.at[1, n]) for n in range(count)]
    for load in loads:
        load.start()
    for load, store in zip(loads, stores):
        load.wait()
        store.start()
    for store in stores:
        store.wait()


def local(outer_size, inner_size, queries, keys, values, d_output):
    rows, width = queries.shape
    groups = width // COLS
    block = jax.ShapeDtypeStruct((rows, width), jnp.bfloat16)
    low, wide = jnp.bfloat16, jnp.float32
    dma = pltpu.SemaphoreType.DMA
    grads = pl.pallas_call(
        functools.partial(kernel, outer_size, inner_size, groups, rows),
        out_shape=(block, block, block),
        in_specs=[pl.BlockSpec(memory_space=pl.ANY)] * 4,
        out_specs=[pl.BlockSpec(memory_space=pl.ANY)] * 3,
        scratch_shapes=[
            pltpu.VMEM((groups, 2, 3, rows, COLS), low),
            pltpu.VMEM((groups, 2, rows, COLS), low),
            pltpu.VMEM((groups, 2, rows, COLS), low),
            pltpu.VMEM((groups, 2, rows, COLS), low),
            pltpu.VMEM((groups, 2, COLS, rows), low),
            pltpu.VMEM((groups, 3, 2, rows, rows), wide),
            pltpu.VMEM((groups, 3, 2, rows, rows), wide),
            pltpu.VMEM((groups, 2, rows, 3 * rows), low),
            pltpu.VMEM((groups, 2, rows, 3 * rows), low),
            pltpu.VMEM((3, groups, 8, rows), wide),
            pltpu.VMEM((3, groups // 2, 8, rows), wide),
            pltpu.VMEM((3, 2, groups // 2, 8, rows), wide),
            pltpu.VMEM((groups, COLS, rows), wide),
            pltpu.VMEM((groups, 2, COLS, rows), low),
            pltpu.VMEM((groups, 2, COLS, rows), low),
            pltpu.VMEM((3, 2, rows, COLS), low),
            pltpu.VMEM((groups, rows, COLS), low),
            pltpu.VMEM((groups, rows, COLS), low),
            pltpu.VMEM((groups, rows, COLS), low),
            dma((3, groups)),
            dma((4, groups)),
            dma((2, groups)), dma((2, groups)),
            dma((6, len(BATCHES))), dma((6, len(BATCHES))),
            dma((2, groups)), dma((2, groups)),
            dma((groups,)), dma((3,)), dma((3,)),
        ],
        compiler_params=pltpu.CompilerParams(
            collective_id=0, has_side_effects=True, vmem_limit_bytes=58 * 2**20),
    )(queries, keys, values, d_output)
    return pl.pallas_call(
        copy_kernel,
        out_shape=(block, block, block),
        in_specs=[pl.BlockSpec(memory_space=pl.ANY)] * 3,
        out_specs=[pl.BlockSpec(memory_space=pl.ANY)] * 3,
        scratch_shapes=[pltpu.VMEM((rows, width), low)] * 3 + [dma((2, 3))],
    )(*grads)


def solution(mesh):
    spec = P(("outer", "inner"), None)
    return jax.shard_map(
        functools.partial(local, mesh.shape["outer"], mesh.shape["inner"]),
        mesh=mesh, in_specs=(spec,) * 4, out_specs=(spec,) * 3, check_vma=False)
```
